32 devices in a mesh: dp: 8 (over z, x), group: 4 (over y, core).
Axes of the slice: x: 2, y: 2, z: 4, core: 2. Of those that a mesh axis runs over, the one named last changes fastest.
Arguments:
- tokens: bfloat16 [24576, 1024], P(('dp', 'group')), may hold values from -6 to 6
- segments: int32 [24576], P('dp'), may hold values from 0 to 2, as said below
- cotangent: bfloat16 [24576, 1024], P(('dp', 'group')), may hold values from -6 to 6
- mixer_master: float32 [1024, 4096], P(('dp', 'group')), may hold values from -0.1875 to 0.1875
- mixer_first: float32 [1024, 4096], P(('dp', 'group')), may hold values from -78.383675 to 78.383675
- mixer_second: float32 [1024, 4096], P(('dp', 'group')), may hold values from 1292.6976 to 5160.96
- ffn_master: float32 [1024, 3, 4608], P(('dp', 'group')), may hold values from -0.1875 to 0.1875
- ffn_first: float32 [1024, 3, 4608], P(('dp', 'group')), may hold values from -39.191837 to 39.191837
- ffn_second: float32 [1024, 3, 4608], P(('dp', 'group')), may hold values from 319.488 to 1302.528
- small_master: float32 [5, 1024], P(None, 'group'), may hold values from 0.25 to 1.75
- small_first: float32 [5, 1024], P(None, 'group'), may hold values from -78.383675 to 78.383675
- small_second: float32 [5, 1024], P(None, 'group'), may hold values from 1292.6976 to 5160.96
Outputs:
- block_out: float32 [24576, 1024], P(('dp', 'group'))
- tokens_grad: float32 [24576, 1024], P(('dp', 'group'))
- mixer_first_new: float32 [1024, 4096], P(('dp', 'group'))
- mixer_second_new: float32 [1024, 4096], P(('dp', 'group'))
- mixer_new: float32 [1024, 4096], P(('dp', 'group'))
- ffn_first_new: float32 [1024, 3, 4608], P(('dp', 'group'))
- ffn_second_new: float32 [1024, 3, 4608], P(('dp', 'group'))
- ffn_new: float32 [1024, 3, 4608], P(('dp', 'group'))
- small_first_new: float32 [5, 1024], P(None, 'group')
- small_second_new: float32 [5, 1024], P(None, 'group')
- small_new: float32 [5, 1024], P(None, 'group')
The draws below stay inside these ranges and needn't reach their ends.
Inputs may be any that keep to these rules, and one draw needn't show every extreme that they name: `segments`: within each sequence of 3072 tokens the numbers are 0, 1, 2 in order; document 1 begins within the first 384 tokens and ends within the last 384 tokens.
All inputs are finite; a program needn't handle non-finite values.
Results may differ from the reference program's by a relative error of at most 0.022.
Values may be sent and summed in bfloat16 or wider, within the bound.
No kernel may reach another device: no remote copies, remote signals or barrier semaphores. Data moves between devices by JAX's collectives and lax.ppermute only.
A program may use at most 256 MiB of HBM per device.

```python
import jax
import jax.numpy as jnp
from jax import lax

D = 1024
FF = 4608
TOK_DEV = 768
STEP = 10
SEQ = 3072
TOKENS = 24576


def draw_segments(key, part):
    key = jax.random.fold_in(key, 7)
    first_key, second_key = jax.random.split(key)
    count_seq = TOKENS // SEQ
    begin = jax.random.randint(first_key, (count_seq, 1), 1, TOK_DEV // 2 + 1)
    finish = jax.random.randint(second_key, (count_seq, 1), SEQ - TOK_DEV // 2, SEQ)
    places = jnp.arange(SEQ, dtype=jnp.int32)[None, :]
    numbers = (places >= begin).astype(jnp.int32) + (places >= finish).astype(jnp.int32)
    return numbers.reshape(-1).astype(jnp.int32)


def with_spikes(drawn, rng, source, target, blocks, factor):
    def block_of(dim):
        return (jnp.arange(drawn.shape[dim]) // (drawn.shape[dim] // blocks)).reshape((-1,) + (1,) * (drawn.ndim - 1 - dim))

    one_side = jax.random.permutation(rng, blocks)[block_of(target)]
    far = (block_of(target) + blocks // 2) % blocks
    return jnp.where((block_of(source) == one_side) | (block_of(source) == far), factor * drawn, drawn)


def block_scale(stream_key, shape, cuts, low, top_value):
    level = 1.0
    for dim, parts in cuts:
        heights = jax.random.uniform(jax.random.fold_in(jax.random.fold_in(stream_key, 6), dim), (parts,), jnp.float32, low / len(cuts), top_value / len(cuts))
        level = level * jnp.repeat(jnp.exp(heights), shape[dim] // parts).reshape((-1,) + (1,) * (len(shape) - 1 - dim))
    return level


def centred(stream_key, shape, spread, bound, shards=(), held_as=jnp.bfloat16):
    factor_of = block_scale(stream_key, shape, shards, -0.22, 0.18) if shards else 1.0
    entries = jax.random.normal(stream_key, shape, jnp.float32) * spread * factor_of
    return jnp.minimum(jnp.maximum(entries, -bound), bound).astype(held_as)


def bell_draw_with(own_key, dims, deviation, limit, cuts, heavy, kind=jnp.bfloat16):
    entries = deviation * jax.random.normal(own_key, dims, jnp.float32)
    if cuts:
        entries = entries * block_scale(own_key, dims, cuts, -0.22, 0.18)
    return jnp.clip(with_spikes(entries, jax.random.fold_in(own_key, 3), *heavy), -limit, limit).astype(kind)


def setup_inputs(seed: int = 0) -> dict:
    arg_keys = jax.random.split(jax.random.key(seed), 13)
    tokens = centred(arg_keys[0], (TOKENS, D), 1.0, 6.0, ((0, 32),))
    segments = draw_segments(jax.random.fold_in(arg_keys[12], 71), 0)
    cotangent = bell_draw_with(arg_keys[2], (TOKENS, D), 1.0, 6.0, ((0, 32),), (0, 1, 32, 2.75))
    mixer_master = centred(arg_keys[3], (D, 4 * D), D ** -0.5, 0.1875, ((0, 32),), jnp.float32)
    mixer_first = centred(arg_keys[4], (D, 4 * D), (0.11 * TOKENS ** 0.5), 78.383675, ((0, 32),), jnp.float32)
    mixer_second = jnp.clip(1292.6976 + 3868.2623 * jax.random.uniform(arg_keys[5], (D, 4 * D), jnp.float32) ** block_scale(arg_keys[5], (D, 4 * D), ((0, 32),), -0.2, 0.2), 1292.6976, 5160.96)
    ffn_master = centred(arg_keys[6], (D, 3, FF), D ** -0.5, 0.1875, ((0, 32),), jnp.float32)
    ffn_first = centred(arg_keys[7], (D, 3, FF), (0.055 * TOKENS ** 0.5), 39.191837, ((0, 32),), jnp.float32)
    ffn_second = jnp.clip(319.488 + 983.0399 * jax.random.uniform(arg_keys[8], (D, 3, FF), jnp.float32) ** block_scale(arg_keys[8], (D, 3, FF), ((0, 32),), -0.2, 0.2), 319.488, 1302.528)
    small_master = jnp.clip(1.0 + 0.15 * jax.random.normal(arg_keys[9], (5, D), jnp.float32), 0.25, 1.75)
    small_first = centred(arg_keys[10], (5, D), (0.11 * TOKENS ** 0.5), 78.383675, ((1, 4),), jnp.float32)
    small_second = jnp.clip(1292.6976 + 3868.2623 * jax.random.uniform(arg_keys[11], (5, D), jnp.float32) ** block_scale(arg_keys[11], (5, D), ((1, 4),), -0.2, 0.2), 1292.6976, 5160.96)
    return {"tokens": tokens, "segments": segments, "cotangent": cotangent, "mixer_master": mixer_master, "mixer_first": mixer_first, "mixer_second": mixer_second, "ffn_master": ffn_master, "ffn_first": ffn_first, "ffn_second": ffn_second, "small_master": small_master, "small_first": small_first, "small_second": small_second}


norm_eps = 1e-06
beta_one = 0.9
beta_two = 0.95
adam_eps = 1e-08
decay_rate = 0.1
rate_matrix = 0.02
rate_small = 1.0

@jax.custom_vjp
def low(v):
    return lax.optimization_barrier(v.astype(jnp.bfloat16)).astype(jnp.float32)

@jax.custom_vjp
def low_back(v):
    return v

def low_keep(v):
    return (low(v), None)

def low_pass(kept, grad):
    return (grad,)

def back_keep(v):
    return (v, None)

def back_low(kept, grad):
    return (low(grad),)
low.defvjp(low_keep, low_pass)
low_back.defvjp(back_keep, back_low)

def matmul(left, right):
    return jnp.dot(left, right, precision=lax.Precision.HIGHEST)

def norm_apply(values, gain):
    scale = lax.rsqrt(lax.optimization_barrier(jnp.mean(values * values, axis=-1, keepdims=True)) + norm_eps)
    return values * scale * gain

def sequence_forward(params, inputs, documents):
    mixer, ffn, small = params
    width = inputs.shape[1]
    length = inputs.shape[0]
    first_in = low(norm_apply(inputs, small[0]))
    projected = low_back(matmul(first_in, mixer[:, :3 * width]))
    first_gate = projected[:, :width]
    output_gate = projected[:, width:2 * width]
    values_in = projected[:, 2 * width:]
    gated_values = low(first_gate * values_in)
    padded = jnp.concatenate([jnp.zeros((2, width), gated_values.dtype), gated_values], axis=0)
    docs_padded = jnp.concatenate([jnp.full((2,), -1, jnp.int32), documents.astype(jnp.int32)])
    convolved = jnp.zeros_like(gated_values)
    for offset in range(3):
        shifted = padded[2 - offset:2 - offset + length]
        same = (docs_padded[2 - offset:2 - offset + length] == documents.astype(jnp.int32)).astype(gated_values.dtype)
        convolved = convolved + small[2 + offset] * shifted * same[:, None]
    convolved = low_back(convolved)
    mixer_in = low(output_gate * convolved)
    mixed = low_back(matmul(mixer_in, mixer[:, 3 * width:]))
    residual = inputs + mixed
    second_in = low(norm_apply(residual, small[1]))
    ffn_gate = low_back(matmul(second_in, ffn[:, 0, :]))
    ffn_up = low_back(matmul(second_in, ffn[:, 1, :]))
    hidden_act = low(jax.nn.silu(ffn_gate) * ffn_up)
    ffn_out = lax.dot_general(hidden_act, ffn[:, 2, :], (((1,), (1,)), ((), ())), precision=lax.Precision.HIGHEST)
    return residual + ffn_out

def adamw(master, first, second, grad, rate, decay):
    first_new = beta_one * first + (1.0 - beta_one) * grad
    second_new = beta_two * second + (1.0 - beta_two) * grad * grad
    fix_one = 1.0 - beta_one ** STEP
    fix_two = 1.0 - beta_two ** STEP
    direction = first_new / fix_one / (jnp.sqrt(second_new / fix_two) + adam_eps)
    return (first_new, second_new, master - rate * (direction + decay * master))

def reference(tokens, segments, cotangent, mixer_master, mixer_first, mixer_second, ffn_master, ffn_first, ffn_second, small_master, small_first, small_second):
    params = (low(mixer_master), low(ffn_master), low(small_master))
    inputs = tokens.astype(jnp.float32)
    count_seq = inputs.shape[0] // SEQ
    sequences = inputs.reshape(count_seq, SEQ, inputs.shape[1])
    documents = segments.astype(jnp.int32).reshape(count_seq, SEQ)

    def whole(params, sequences):

        def one(pair):
            return sequence_forward(params, pair[0], pair[1])
        return lax.map(jax.checkpoint(one), (sequences, documents))
    outputs, pullback = jax.vjp(whole, params, sequences)
    back = cotangent.astype(jnp.float32).reshape(count_seq, SEQ, inputs.shape[1])
    grads, input_grads = pullback(back)
    mixer_grad, ffn_grad, small_grad = grads
    mixer_f, mixer_s, mixer_n = adamw(mixer_master, mixer_first, mixer_second, mixer_grad, rate_matrix, decay_rate)
    ffn_f, ffn_s, ffn_n = adamw(ffn_master, ffn_first, ffn_second, ffn_grad, rate_matrix, decay_rate)
    small_f, small_s, small_n = adamw(small_master, small_first, small_second, small_grad, rate_small, 0.0)
    block_out = outputs.reshape(inputs.shape)
    tokens_grad = input_grads.reshape(inputs.shape)
    return (block_out, tokens_grad, mixer_f, mixer_s, mixer_n, ffn_f, ffn_s, ffn_n, small_f, small_s, small_n)
```

```python
import functools

import jax
import jax.numpy as jnp
from jax import lax
from jax.experimental import pallas as pl
from jax.experimental.pallas import tpu as pltpu
from jax.sharding import PartitionSpec as P

STEP = 10

norm_eps = 1e-06
beta_one = 0.9
beta_two = 0.95
adam_eps = 1e-08
decay_rate = 0.1
rate_matrix = 0.02
rate_small = 1.0

MIB = 1 << 20
ORDER = ((0, 5), (0, 10), (3, 10), (29, 30), (26, 34), (37, 43), (40, 43), (39, 46), (50, 51), (40, 56), (44, 57), (40, 63), (61, 65), (56, 66), (62, 70), (53, 74), (68, 74), (72, 75), (79, 83))
OFF = ((3, 2), (4, 0), (5, 0), (12, 0), (15, 2), (17, 0), (19, 0))
trace = None
VMEM = 60
WEIGHT = 0.001
BF16 = jnp.bfloat16
F32 = jnp.float32
GROUP = 4
NEAR, FAR = 1, 2


def shape_of(shape, dtype):
    return jax.ShapeDtypeStruct(tuple(shape), dtype)


def dot_rows(left, right):
    return lax.dot_general(left, right, (((0,), (0,)), ((), ())), preferred_element_type=F32)


def dot_cols(left, right):
    return lax.dot_general(left, right, (((1,), (1,)), ((), ())), preferred_element_type=F32)


def dot(left, right):
    return jnp.dot(left, right, preferred_element_type=F32)


def adamw(master, first, second, grad, rate, decay):
    first_new = beta_one * first + (1.0 - beta_one) * grad
    second_new = beta_two * second + (1.0 - beta_two) * grad * grad
    fix_one = 1.0 - beta_one**STEP
    fix_two = 1.0 - beta_two**STEP
    direction = first_new / fix_one / (jnp.sqrt(second_new / fix_two) + adam_eps)
    return (first_new, second_new, master - rate * (direction + decay * master))


class Trace:
    def __init__(self):
        self.results = []
        self.holds = 0

    def ready(self, operand):
        step = len(self.results)
        earlier = [self.results[j] for j, i in ORDER if i == step and j < step]
        return lax.optimization_barrier([operand] + earlier)[0] if earlier else operand

    def done(self, results):
        self.results.append(jax.tree.leaves(results)[0])
        return results


def swapped(block, axis, distance):
    pairs = [(i, i ^ distance) for i in range(lax.axis_size(axis))]
    return trace.done(lax.ppermute(trace.ready(block), axis, pairs))


def after(values, *others):
    hold = trace.holds
    trace.holds += 1
    others = tuple(o for j, o in enumerate(others) if (hold, j) not in OFF)
    return lax.optimization_barrier((values,) + others)[0] if others else values


def call(
    kernel, name, out_shape, *, where, grid=(), in_specs, out_specs, scratch=(), flops, moved, aliases={}
):
    run = pl.pallas_call(
        kernel,
        out_shape=out_shape,
        grid_spec=pltpu.PrefetchScalarGridSpec(
            num_scalar_prefetch=1,
            grid=grid,
            in_specs=in_specs,
            out_specs=out_specs,
            scratch_shapes=scratch,
        ),
        compiler_params=pltpu.CompilerParams(
            vmem_limit_bytes=VMEM * MIB,
            dimension_semantics=("arbitrary",) * len(grid) if grid else None,
        ),
        cost_estimate=pl.CostEstimate(
            flops=int(flops * WEIGHT), bytes_accessed=int(moved * WEIGHT), transcendentals=0
        ),
        input_output_aliases=aliases,
        name=name,
    )
    return lambda first, *rest: trace.done(run(where, trace.ready(first), *rest))


def whole(array):
    rank = len(array.shape)
    return pl.BlockSpec(tuple(array.shape), lambda *_: (0,) * rank)


def wholes(arrays):
    return [whole(a) for a in arrays]


def untouched():
    return pl.BlockSpec(memory_space=pl.ANY)


def send_kernel(where, mixer, ffn, small, *outs, part, hpart, chunks):
    me = where[0]
    base = 4 * part
    last = base + 3 * hpart
    for k in range(GROUP):
        out = outs[k]
        for j in range(4):
            start = pl.multiple_of((me ^ k) * part + j * GROUP * part, part)
            out[:, j * part : (j + 1) * part] = mixer[:, pl.ds(start, part)].astype(BF16)
        for first, size in chunks:
            start = pl.multiple_of((me ^ k) * hpart + first, 128)
            for j in range(3):
                at = base + 3 * first + j * size
                out[:, at : at + size] = ffn[j, :, pl.ds(start, size)].astype(BF16)
        pad = jnp.zeros((out.shape[0] - small.shape[0], part), F32)
        out[:, last:] = jnp.concatenate([small[...], pad], axis=0).astype(BF16)


def take_kernel(where, *refs, part, hpart, chunks):
    blocks, (mixer, small), ffns = refs[:GROUP], refs[GROUP : GROUP + 2], refs[GROUP + 2 :]
    base = 4 * part
    last = base + 3 * hpart
    for k in range(GROUP):
        source = where[0] ^ k
        mixer[source] = blocks[k][:, :base]
        for out, (first, size) in zip(ffns, chunks):
            out[source] = blocks[k][:, base + 3 * first : base + 3 * (first + size)]
        small[:, pl.ds(pl.multiple_of(source * part, part), part)] = blocks[k][:, last:].astype(F32)[
            :8
        ]


def out_stack_kernel(where, *refs, start, size):
    pieces, (out, sems) = refs[:-2], refs[-2:]
    fetch_rows(where, pieces, out, sems, start, size)


def fetch_rows(where, pieces, target, sems, first, cols):
    rows = pieces[0].shape[0]
    copies = [
        pltpu.make_async_copy(
            piece.at[:, pl.ds(first, cols)],
            target.at[pl.ds(pl.multiple_of((where[1] ^ e) * rows, 32), rows), :],
            sems.at[e],
        )
        for e, piece in enumerate(pieces)
    ]
    for copy in copies:
        copy.start()
    for copy in copies:
        copy.wait()


def same_document(where, place, lag):
    same = place >= lag
    for begin in (where[2], where[3]):
        same = jnp.logical_and(same, jnp.logical_or(place < begin, place >= begin + lag))
    return same


def mixer_in_kernel(where, *refs, count, tiles, part):
    tokens, small, refs = refs[:GROUP], refs[GROUP], refs[GROUP + 1 :]
    pieces, refs = refs[:count], refs[count:]
    first_in, projected, convolved, mixer_in, w_in, held, carry, sems = refs
    step = pl.program_id(0)
    me = where[0]

    @pl.when(step == 0)
    def _():
        fetch_rows(where, pieces, w_in, sems, 0, 3 * part)
        carry[...] = jnp.zeros_like(carry)

    for k in range(GROUP):

        @pl.when((step // tiles) ^ me == k)
        def _(k=k):
            held[...] = tokens[k][...]

    inputs = held[...].astype(F32)
    scale = lax.rsqrt(jnp.mean(inputs * inputs, axis=-1, keepdims=True) + norm_eps)
    normed = (inputs * scale * small[0:1, :]).astype(BF16)
    first_in[...] = normed
    columns = dot(normed, w_in[...])
    projected[...] = columns
    gated = (columns[:, :part] * columns[:, 2 * part :]).astype(BF16).astype(F32)
    taps = small[2:5, pl.ds(pl.multiple_of(me * part, part), part)]
    row = lax.broadcasted_iota(jnp.int32, gated.shape, 0)
    before = carry[...]
    one = jnp.where(row == 0, before[7:8], pltpu.roll(gated, 1, 0))
    two = jnp.where(
        row == 0, before[6:7], jnp.where(row == 1, before[7:8], pltpu.roll(gated, 2, 0))
    )
    carry[...] = gated[gated.shape[0] - 8 :]
    place = row + step * gated.shape[0]
    one = jnp.where(same_document(where, place, 1), one, 0.0)
    two = jnp.where(same_document(where, place, 2), two, 0.0)
    mixed = taps[0:1] * gated + taps[1:2] * one + taps[2:3] * two
    convolved[...] = mixed
    mixer_in[...] = (columns[:, part : 2 * part] * mixed).astype(BF16)


def residual_kernel(where, *refs, tiles, part):
    tokens, mixer_in, refs = refs[:GROUP], refs[GROUP : 2 * GROUP], refs[2 * GROUP :]
    small, slices, refs = refs[0], refs[1 : 1 + GROUP], refs[1 + GROUP :]
    second_in, residual_out, mixer_own, w_out, held, inputs_held, sems = refs
    step = pl.program_id(0)
    columns = [pl.ds(pl.multiple_of((where[0] ^ k) * part, part), part) for k in range(GROUP)]

    @pl.when(step == 0)
    def _():
        copies = [
            pltpu.make_async_copy(slices[k], w_out.at[:, columns[k]], sems.at[k])
            for k in range(GROUP)
        ]
        for copy in copies:
            copy.start()
        for copy in copies:
            copy.wait()

    for k in range(GROUP):
        held[:, columns[k]] = mixer_in[k][...]

        @pl.when(step // tiles == k)
        def _(k=k):
            inputs_held[...] = tokens[k][...]

    residual = inputs_held[...].astype(F32) + dot(held[...], w_out[...])
    scale = lax.rsqrt(jnp.mean(residual * residual, axis=-1, keepdims=True) + norm_eps)
    second_in[...] = (residual * scale * small[1:2, :]).astype(BF16)

    @pl.when(step < tiles)
    def _():
        residual_out[...] = residual
        mixer_own[...] = held[...]


def ffn_kernel(where, *refs, tiles, part):
    many = 2 * tiles
    second_in, cots, source, refs = refs[0], refs[1 : 1 + many], refs[1 + many], refs[-11:]
    act_out, gate_out, up_out, cot_out, out_a, out_b, back_a, back_b, weights, held, sem = refs
    step = pl.program_id(0)

    @pl.when(step == 0)
    def _():
        copy = pltpu.make_async_copy(source, weights, sem)
        copy.start()
        copy.wait()

    for k in range(many):

        @pl.when(step == k)
        def _(k=k):
            held[...] = cots[k][...]

    normed = second_in[...]
    cotangent = held[...]
    cot_out[...] = cotangent
    for first in range(0, part, 256):
        size = min(256, part - first)
        gate = dot(normed, weights[:, first : first + size])
        up = dot(normed, weights[:, part + first : part + first + size])
        grad_act = dot(cotangent, weights[:, 2 * part + first : 2 * part + first + size])
        sig = 0.5 * jnp.tanh(0.5 * gate) + 0.5
        swish = gate * sig
        act_out[:, first : first + size] = (swish * up).astype(BF16)
        gate_out[:, first : first + size] = (
            grad_act * up * (sig * (1.0 + gate * (1.0 - sig)))
        ).astype(BF16)
        up_out[:, first : first + size] = (grad_act * swish).astype(BF16)
    out = dot_cols(act_out[...], weights[:, 2 * part :]).astype(BF16)
    back = (
        dot_cols(gate_out[...], weights[:, :part])
        + dot_cols(up_out[...], weights[:, part : 2 * part])
    ).astype(BF16)

    @pl.when(step < tiles)
    def _():
        out_a[...] = out
        back_a[...] = back

    @pl.when(step >= tiles)
    def _():
        out_b[...] = out
        back_b[...] = back


def weight_grad_kernel(where, *refs, lefts, rights, plan, rows, extra):
    left_refs, right_refs, refs = refs[:lefts], refs[lefts : lefts + rights], refs[lefts + rights :]
    if extra:
        (more,), refs = refs[:1], refs[1:]
    many = len(plan[0][2])
    outs, (left_held, right_held, total, sems) = refs[: 2 * many], refs[2 * many :]
    cols = total.shape[2]
    dp = where[1]

    def copies(at):
        left, left_start, sides, size = plan[at]
        slot = at % 2
        return [
            pltpu.make_async_copy(
                left_refs[left].at[pl.ds(left_start, size), :], left_held.at[slot], sems.at[0, slot]
            )
        ] + [
            pltpu.make_async_copy(
                right_refs[right].at[pl.ds(start, size), :],
                right_held.at[slot, m],
                sems.at[1 + m, slot],
            )
            for m, (right, start) in enumerate(sides)
        ]

    for copy in copies(0):
        copy.start()
    for at in range(len(plan)):
        if at + 1 < len(plan):
            for copy in copies(at + 1):
                copy.start()
        for copy in copies(at):
            copy.wait()
        left = left_held[at % 2]
        for m in range(many):
            part = dot_rows(left, right_held[at % 2, m])
            total[m] = part if at == 0 else total[m] + part
    for m in range(many):
        mine, theirs = outs[2 * m : 2 * m + 2]
        for j in range(mine.shape[0]):
            for target, side in ((mine, dp % 2), (theirs, 1 - dp % 2)):
                place = pl.multiple_of((2 * (j ^ (dp // 2)) + side) * rows, 32)
                target[j, :, :cols] = total[m, pl.ds(place, rows), :].astype(BF16)
                if extra:
                    target[j, :, cols:] = more[pl.ds(place, rows), :]


def out_grad_kernel(where, left, right, *refs, part):
    outs, held = refs[:GROUP], refs[GROUP]
    held[...] = dot_rows(left[...], right[...])
    for k in range(GROUP):
        outs[k][...] = held[:, pl.ds(pl.multiple_of((where[0] ^ k) * part, part), part)].astype(BF16)


def first_halve_kernel(where, mine_keep, mine_send, got_keep, got_send, keep, send):
    keep[...] = (mine_keep[...].astype(F32) + got_keep[...].astype(F32)).astype(BF16)
    send[...] = (mine_send[...].astype(F32) + got_send[...].astype(F32)).astype(BF16)


def halve_kernel(where, mine, got, keep, send):
    for j in range(keep.shape[0]):
        keep[j] = (mine[2 * j].astype(F32) + got[2 * j].astype(F32)).astype(BF16)
        send[j] = (mine[2 * j + 1].astype(F32) + got[2 * j + 1].astype(F32)).astype(BF16)


def finish_sum_kernel(where, *refs, terms, owned):
    outs, held = refs[-GROUP - 1 : -1], refs[-1]
    at = 0
    place = 0
    cols = held.shape[2]
    for many in terms:
        for first in range(0, refs[at].shape[1], cols):
            total = refs[at][:, first : first + cols].astype(F32)
            for other in refs[at + 1 : at + many]:
                total = total + other[:, first : first + cols].astype(F32)
            held[...] = total.reshape(held.shape)
            for k in range(GROUP):
                outs[k][place] = held[where[0] ^ k].astype(BF16)
            place += 1
        at += many


def residual_back_kernel(where, g0, g1, g2, residual, cotangent, small, w_out, *refs, part):
    grad_out, mixed_out, gain, outs, held = refs[0], refs[1], refs[2], refs[3:6], refs[6]
    grad = g0[...].astype(F32) + g1[...].astype(F32) + g2[...].astype(F32)
    values = residual[...]
    scale = lax.rsqrt(jnp.mean(values * values, axis=-1, keepdims=True) + norm_eps)
    normed = values * scale
    hat = grad * small[1:2, :]
    grad_in = cotangent[...].astype(F32) + scale * (
        hat - normed * jnp.mean(hat * normed, axis=-1, keepdims=True)
    )
    grad_out[...] = grad_in
    mixed = grad_in.astype(BF16)
    mixed_out[...] = mixed

    @pl.when(pl.program_id(0) == 0)
    def _():
        gain[...] = jnp.zeros_like(gain)

    gain[...] += jnp.sum(grad * normed, axis=0, keepdims=True)
    held[...] = dot_cols(mixed, w_out[...]).astype(BF16)
    for k in range(GROUP):
        columns = held[:, pl.ds(pl.multiple_of((where[0] ^ k) * part, part), part)]
        if k < FAR:
            outs[k][...] = columns
        else:
            outs[FAR][:, (k - FAR) * part : (k - FAR + 1) * part] = columns


def mixer_back_kernel(where, *refs, tiles, part):
    grads, tokens, refs = refs[:GROUP], refs[GROUP : 2 * GROUP], refs[2 * GROUP :]
    (projected, convolved, small, w_in), refs = refs[:4], refs[4:]
    grad_proj, tap_terms, gain, outs, (held, tokens_held, carry) = (
        refs[0],
        refs[1],
        refs[2],
        refs[3 : 3 + GROUP],
        refs[3 + GROUP :],
    )
    step = pl.program_id(0)
    me = where[0]
    which = ((pl.num_programs(0) - 1 - step) // tiles) ^ me

    @pl.when(step == 0)
    def _():
        carry[...] = jnp.zeros_like(carry)
        tap_terms[...] = jnp.zeros_like(tap_terms)
        gain[...] = jnp.zeros_like(gain)

    for k in range(GROUP):

        @pl.when(which == k)
        def _(k=k):
            held[...] = grads[k][...]
            tokens_held[...] = tokens[k][...]

    grad_mixer_in = held[...].astype(F32)
    first_gate = projected[:, :part]
    output_gate = projected[:, part : 2 * part]
    values_in = projected[:, 2 * part :]
    gated = (first_gate * values_in).astype(BF16).astype(F32)
    grad_conv = (grad_mixer_in * output_gate).astype(BF16).astype(F32)
    grad_output = grad_mixer_in * convolved[...]
    size = grad_conv.shape[0]
    row = lax.broadcasted_iota(jnp.int32, grad_conv.shape, 0)
    behind = carry[...]
    one = jnp.where(row == size - 1, behind[0:1], pltpu.roll(grad_conv, size - 1, 0))
    two = jnp.where(
        row == size - 1,
        behind[1:2],
        jnp.where(row == size - 2, behind[0:1], pltpu.roll(grad_conv, size - 2, 0)),
    )
    carry[...] = grad_conv[:8]
    place = row + (pl.num_programs(0) - 1 - step) * size
    last = pl.num_programs(0) * size
    one = jnp.where(jnp.logical_and(same_document(where, place + 1, 1), place + 1 < last), one, 0.0)
    two = jnp.where(jnp.logical_and(same_document(where, place + 2, 2), place + 2 < last), two, 0.0)
    taps = small[2:5, pl.ds(pl.multiple_of(me * part, part), part)]
    grad_gated = taps[0:1] * grad_conv + taps[1:2] * one + taps[2:3] * two
    tap_terms[0:1, :] += jnp.sum(grad_conv * gated, axis=0, keepdims=True)
    tap_terms[1:2, :] += jnp.sum(one * gated, axis=0, keepdims=True)
    tap_terms[2:3, :] += jnp.sum(two * gated, axis=0, keepdims=True)
    grad_proj[:, :part] = (grad_gated * values_in).astype(BF16)
    grad_proj[:, part : 2 * part] = grad_output.astype(BF16)
    grad_proj[:, 2 * part :] = (grad_gated * first_gate).astype(BF16)
    grad_first = dot_cols(grad_proj[...], w_in[...])
    inputs = tokens_held[...].astype(F32)
    scale = lax.rsqrt(jnp.mean(inputs * inputs, axis=-1, keepdims=True) + norm_eps)
    gain[...] += jnp.sum(grad_first * (inputs * scale), axis=0, keepdims=True)
    rounded = grad_first.astype(BF16)
    for k in range(GROUP):

        @pl.when(which == k)
        def _(k=k):
            outs[k][...] = rounded


def tokens_grad_kernel(where, g0, g1, g2, tokens, grad_resid, small, out):
    grad = g0[...].astype(F32) + g1[...].astype(F32) + g2[...].astype(F32)
    values = tokens[...].astype(F32)
    scale = lax.rsqrt(jnp.mean(values * values, axis=-1, keepdims=True) + norm_eps)
    normed = values * scale
    hat = grad * small[0:1, :]
    out[...] = grad_resid[...] + scale * (
        hat - normed * jnp.mean(hat * normed, axis=-1, keepdims=True)
    )


def mixer_adam_kernel(where, g0, g1, g2, g3, master, first, second, first_out, second_out, new_out, held, *, part):
    for k, grad in enumerate((g0, g1, g2, g3)):
        for j in range(4):
            start = (where[0] ^ k) * part + j * GROUP * part
            held[:, pl.ds(pl.multiple_of(start, part), part)] = grad[
                :, j * part : (j + 1) * part
            ].astype(F32)
    first_out[...], second_out[...], new_out[...] = adamw(
        master[...], first[...], second[...], held[...], rate_matrix, decay_rate
    )


def ffn_adam_kernel(where, g0, g1, g2, g3, master, first, second, first_out, second_out, new_out, held, *, part):
    for k, grad in enumerate((g0, g1, g2, g3)):
        start = pl.multiple_of((where[0] ^ k) * part, 128)
        held[:, pl.ds(start, part)] = grad[...].astype(F32)
    first_out[0], second_out[0], new_out[0] = adamw(
        master[0], first[0], second[0], held[...], rate_matrix, decay_rate
    )


def local(
    tokens,
    segments,
    cotangent,
    mixer_master,
    mixer_first,
    mixer_second,
    ffn_master,
    ffn_first,
    ffn_second,
    small_master,
    small_first,
    small_second,
):
    global trace
    trace = Trace()
    length, width = tokens.shape
    hidden = ffn_master.shape[2]
    owned = mixer_master.shape[0]
    count = lax.axis_size("dp")
    sequence = GROUP * length
    part = width // GROUP
    hpart = hidden // GROUP
    rows = GROUP * owned
    tile = length // 2
    tiles = length // tile
    steps = sequence // tile
    chunks = ((0, hpart),)
    where = jnp.stack([lax.axis_index("group"), lax.axis_index("dp")]).astype(jnp.int32)

    def group_gathered(own, *order, then=()):
        far = swapped(after(own, *order) if order else own, "group", FAR)
        near = swapped(own, "group", NEAR)
        return [own, near, far, swapped(after(far, *then) if then else far, "group", NEAR)]

    ffn_flat = ffn_master.transpose(1, 0, 2)
    send = [shape_of((owned, 4 * part + 3 * hpart + part), BF16)] * GROUP
    blocks = call(
        functools.partial(send_kernel, part=part, hpart=hpart, chunks=chunks),
        "send",
        send,
        where=where,
        in_specs=wholes([mixer_master, ffn_flat, small_master]),
        out_specs=wholes(send),
        flops=0,
        moved=owned * (width * 24 + hidden * 18),
    )(mixer_master, ffn_flat, small_master)
    blocks = [blocks[0]] + [swapped(blocks[k], "group", k) for k in range(1, GROUP)]
    take = [shape_of((GROUP, owned, 4 * part), BF16), shape_of((8, width), F32)]
    take += [shape_of((GROUP, owned, 3 * size), BF16) for _, size in chunks]
    mixer_rows, small_all, *ffn_rows = call(
        functools.partial(take_kernel, part=part, hpart=hpart, chunks=chunks),
        "take",
        take,
        where=where,
        in_specs=wholes(blocks),
        out_specs=wholes(take),
        flops=0,
        moved=owned * (width * 16 + hidden * 12),
    )(*blocks)
    far = count // 2

    def z_stages(own):
        pieces = {0: own}
        for e in sorted(range(2, count, 2), key=lambda e: (e.bit_count(), -e)):
            source = pieces[e & (e - 1)]
            pieces[e] = swapped(source, "dp", e & -e)
        return pieces

    mixer_own_rows = mixer_rows.reshape(rows, 4 * part)
    ffn_own_rows = [block.reshape(rows, block.shape[2]) for block in ffn_rows]
    mixer_z = z_stages(mixer_own_rows)
    mixer_near = swapped(mixer_own_rows, "dp", 1)
    mixer_z = lax.optimization_barrier([mixer_z[e] for e in range(2, count, 2)] + [mixer_near])
    mixer_z = mixer_z[: far - 1]
    ffn_cols = lax.all_gather(
        lax.optimization_barrier((ffn_own_rows[0], mixer_z[0], mixer_z[1]))[0], "dp", axis=0, tiled=True
    )
    mixer_x = [swapped(block, "dp", 1) for block in mixer_z]
    mixer_pieces = [mixer_own_rows, mixer_near]
    for block, other in zip(mixer_z, mixer_x):
        mixer_pieces += [block, other]

    tokens_far = swapped(after(tokens, *blocks[1:]), "group", FAR)
    tokens_of = [tokens, swapped(tokens, "group", NEAR), tokens_far]
    tokens_of += [swapped(after(tokens_far, *mixer_x), "group", NEAR)]

    begins = jnp.sum(
        segments[None, :] < jnp.array([[1], [2]], segments.dtype), axis=1, dtype=jnp.int32
    )
    where = jnp.concatenate([where, begins])

    out_stack = shape_of((width, part), BF16)
    out_stacked = call(
        functools.partial(out_stack_kernel, start=3 * part, size=part),
        "stack",
        out_stack,
        where=where,
        in_specs=[untouched()] * count,
        out_specs=whole(out_stack),
        scratch=[pltpu.SemaphoreType.DMA((count,))],
        flops=0,
        moved=width * part * 4,
    )(*mixer_pieces)
    out_slices = [out_stacked, swapped(out_stacked, "group", NEAR), swapped(out_stacked, "group", FAR)]

    def in_block(k, backward=False):
        def place(step, where):
            at = (steps - 1 - step) if backward else step
            return (jnp.clip(at - (where[0] ^ k) * tiles, 0, tiles - 1), 0)

        return place

    outs = [
        shape_of((sequence, width), BF16),
        shape_of((sequence, 3 * part), F32),
        shape_of((sequence, part), F32),
        shape_of((sequence, part), BF16),
        shape_of((width, 3 * part), BF16),
    ]
    forward = lambda s: pl.BlockSpec((tile, s.shape[1]), lambda i, w: (i, 0))
    first_in, projected, convolved, mixer_in, w_in = call(
        functools.partial(mixer_in_kernel, count=count, tiles=tiles, part=part),
        "mixer_in",
        outs,
        where=where,
        grid=(steps,),
        in_specs=[pl.BlockSpec((tile, width), in_block(k)) for k in range(GROUP)]
        + [whole(small_all)]
        + [untouched()] * count,
        out_specs=[forward(s) for s in outs[:4]] + [whole(outs[4])],
        scratch=[
            pltpu.VMEM((tile, width), BF16),
            pltpu.VMEM((8, part), F32),
            pltpu.SemaphoreType.DMA((count,)),
        ],
        flops=2 * sequence * width * 3 * part,
        moved=sequence * width * 8,
    )(*tokens_of, after(small_all, out_stacked), *mixer_pieces)
    out_slices += [swapped(out_slices[2], "group", NEAR)]
    mixer_in_of = group_gathered(after(mixer_in, out_slices[2]), then=out_slices)

    block_b = shape_of((length, width), BF16)
    outs = [
        shape_of((sequence, width), BF16),
        shape_of((length, width), F32),
        block_b,
        shape_of((width, width), BF16),
    ]
    own_block = pl.BlockSpec((tile, width), lambda i, w: (jnp.minimum(i, tiles - 1), 0))
    second_in, residual, mixer_own, w_out = call(
        functools.partial(residual_kernel, tiles=tiles, part=part),
        "residual",
        outs,
        where=where,
        grid=(steps,),
        in_specs=[
            pl.BlockSpec((tile, width), lambda i, w, k=k: (jnp.clip(i - k * tiles, 0, tiles - 1), 0))
            for k in range(GROUP)
        ]
        + [
            pl.BlockSpec((tile, part), lambda i, w: ((w[0] ^ (i // tiles)) * tiles + i % tiles, 0))
        ]
        * GROUP
        + [whole(small_all)]
        + [untouched()] * GROUP,
        out_specs=[forward(outs[0]), own_block, own_block, whole(outs[3])],
        scratch=[
            pltpu.VMEM((tile, width), BF16),
            pltpu.VMEM((tile, width), BF16),
            pltpu.SemaphoreType.DMA((GROUP,)),
        ],
        flops=2 * sequence * width * width,
        moved=sequence * width * 8,
    )(*tokens_of, *mixer_in_of, small_all, *out_slices)

    low = pl.BlockSpec((tile, width), lambda i, w: (jnp.minimum(i, tiles - 1), 0))
    high = pl.BlockSpec((tile, width), lambda i, w: (jnp.maximum(i - tiles, 0), 0))

    wholes_b = [shape_of((sequence, hpart), BF16)] * 3 + [shape_of((sequence, width), BF16)]

    def ffn_call(second_in, begin, cots, name, kept=()):
        at_tile = lambda s: pl.BlockSpec((tile, s.shape[1]), lambda i, w: (i + begin, 0))
        return call(
            functools.partial(ffn_kernel, tiles=tiles, part=hpart),
            name,
            wholes_b + [block_b] * 4,
            where=where,
            grid=(2 * tiles,),
            in_specs=[at_tile(second_in)]
            + [pl.BlockSpec((tile, width), lambda i, w, at=at: (at, 0)) for _, at in cots]
            + [untouched()] * (1 + len(kept)),
            out_specs=[at_tile(s) for s in wholes_b] + [low, high] * 2,
            scratch=[
                pltpu.VMEM((width, 3 * hpart), BF16),
                pltpu.VMEM((tile, width), BF16),
                pltpu.SemaphoreType.DMA(()),
            ],
            flops=24 * length * width * hpart,
            moved=2 * length * (hpart * 6 + width * 8) + width * hpart * 6,
            aliases={3 + len(cots) + j: j for j in range(len(kept))},
        )(second_in, *[cot for cot, _ in cots], ffn_cols, *kept)

    def for_far(mine, near):
        got = swapped(near, "group", NEAR)
        return (mine.astype(F32) + got.astype(F32)).astype(BF16)

    cotangent_near = swapped(cotangent, "group", NEAR)
    cotangent_far = swapped(after(cotangent, mixer_in_of[2]), "group", FAR)
    *kept, out_0, out_1, back_0, back_1 = ffn_call(
        second_in,
        0,
        [(block, at) for block in (cotangent, cotangent_near) for at in range(tiles)],
        "ffn_own",
    )
    cotangent_far = [
        cotangent_far,
        swapped(lax.optimization_barrier((cotangent_far, kept[0]))[0], "group", NEAR),
    ]
    hidden_act, grad_gate, grad_up, cotangents, out_2, out_3, back_2, back_3 = ffn_call(
        second_in,
        2 * tiles,
        [(block, at) for block in cotangent_far for at in range(tiles)],
        "ffn_far",
        kept,
    )
    back_near = swapped(back_1, "group", NEAR)
    back_sum = for_far(back_2, back_3)
    back_got = swapped(back_sum, "group", FAR)
    out_sum = for_far(out_2, out_3)
    out_near = swapped(out_1, "group", NEAR)

    def weight_grad(lefts, rights, plan, name, more=None):
        cols = rights[0].shape[1]
        many = len(plan[0][2])
        size = plan[0][3]
        out = shape_of(
            (count // 2, rows, cols + (more.shape[1] if more is not None else 0)), BF16
        )
        return call(
            functools.partial(
                weight_grad_kernel,
                lefts=len(lefts),
                rights=len(rights),
                plan=tuple(plan),
                rows=rows,
                extra=more is not None,
            ),
            name,
            [out] * (2 * many),
            where=where,
            in_specs=[untouched()] * (len(lefts) + len(rights))
            + ([whole(more)] if more is not None else []),
            out_specs=wholes([out] * (2 * many)),
            scratch=[
                pltpu.VMEM((2, size, width), BF16),
                pltpu.VMEM((2, many, size, cols), BF16),
                pltpu.VMEM((many, width, cols), F32),
                pltpu.SemaphoreType.DMA((1 + many, 2)),
            ],
            flops=2 * sequence * width * cols * many,
            moved=sequence * (width + cols * many) * 2,
        )(*lefts, *rights, *([more] if more is not None else []))

    def with_theirs(left, right):
        grad = dot_rows(left, right).astype(BF16)
        blocks = grad.reshape(count // 2, 2, rows, grad.shape[1])
        return grad, lax.dynamic_index_in_dim(blocks, 1 - where[1] % 2, 1, keepdims=False)

    gate_grad, gate_theirs = with_theirs(second_in, after(grad_gate, back_sum, back_near))
    gate_got = swapped(gate_theirs, "dp", 1)
    down_grad, down_theirs = with_theirs(cotangents, after(hidden_act, gate_grad))
    up_grad, up_theirs = with_theirs(second_in, after(grad_up, down_grad))

    def to_owners(matrices, name):
        cols = matrices[0][0].shape[1]
        parts = [part for parts in matrices for part in parts]
        blocks_out = shape_of((sum(p[0].shape[1] for p in matrices) // cols, owned, cols), BF16)
        blocks = call(
            functools.partial(
                finish_sum_kernel, terms=tuple(len(parts) for parts in matrices), owned=owned
            ),
            name + "_finish",
            [blocks_out] * GROUP,
            where=where,
            in_specs=wholes(parts),
            out_specs=[whole(blocks_out)] * GROUP,
            scratch=[pltpu.VMEM((GROUP, owned, cols), F32)],
            flops=0,
            moved=rows * cols * 2 * (len(parts) + 1),
        )(*parts)
        return [blocks[0]] + [swapped(blocks[k], "group", k) for k in range(1, GROUP)]

    def halved(mine, got, name):
        half = shape_of((mine.shape[0] // 2,) + mine.shape[1:], BF16)
        return call(
            halve_kernel,
            name,
            [half, half],
            where=where,
            in_specs=wholes([mine, got]),
            out_specs=wholes([half, half]),
            flops=0,
            moved=mine.size * 6,
        )(mine, got)

    def first_halved(grad, got, name):
        cols = grad.shape[1]
        half = shape_of((count // 4, rows, cols), BF16)

        def mine(bit):
            return pl.BlockSpec(
                (rows, cols),
                lambda j, w: (2 * ((2 * j + bit) ^ (w[1] // 2)) + w[1] % 2, 0),
            )

        def theirs(bit):
            return pl.BlockSpec(
                (None, rows, cols), lambda j, w: ((2 * j + bit) ^ (w[1] // 2), 0, 0)
            )

        out = pl.BlockSpec((None, rows, cols), lambda j, w: (j, 0, 0))
        return call(
            first_halve_kernel,
            name,
            [half, half],
            where=where,
            grid=(count // 4,),
            in_specs=[mine(0), mine(1), theirs(0), theirs(1)],
            out_specs=[out, out],
            flops=0,
            moved=grad.size * 3,
        )(grad, grad, got, got)

    def z_summed(keep, send, name):
        distance = 2
        got = swapped(send, "dp", distance)
        while keep.shape[0] > 1:
            keep, send = halved(keep, got, name)
            distance *= 2
            got = swapped(send, "dp", distance)
        return [keep.reshape(keep.shape[1:]), got.reshape(got.shape[1:])]

    block_f = shape_of((length, width), F32)
    row_f = shape_of((1, width), F32)
    slice_b = shape_of((length, part), BF16)
    pair_b = shape_of((length, 2 * part), BF16)
    by_tile = lambda s: pl.BlockSpec((tile, s.shape[1]), lambda i, w: (i, 0))
    grad_resid, grad_mixed, gain_two, *mixer_sent = call(
        functools.partial(residual_back_kernel, part=part),
        "residual_back",
        [block_f, block_b, row_f, slice_b, slice_b, pair_b],
        where=where,
        grid=(tiles,),
        in_specs=[by_tile(s) for s in (block_b, block_b, block_b, block_f, block_b)]
        + wholes([small_all, w_out]),
        out_specs=[by_tile(block_f), by_tile(block_b), whole(row_f)]
        + [by_tile(s) for s in (slice_b, slice_b, pair_b)],
        scratch=[pltpu.VMEM((tile, width), BF16)],
        flops=2 * length * width * width,
        moved=length * width * 20,
    )(after(back_0, up_grad, out_near), back_near, back_got, residual, cotangent, small_all, w_out)
    mixer_got_far = swapped(mixer_sent[2], "group", FAR)
    mixer_got_other = swapped(mixer_sent[1], "group", NEAR)
    cols_b = shape_of((width, part), BF16)
    w_out_parts = call(
        functools.partial(out_grad_kernel, part=part),
        "out_grad",
        [cols_b] * GROUP,
        where=where,
        grid=(width // 256,),
        in_specs=[pl.BlockSpec((length, 256), lambda i, w: (0, i)), whole(block_b)],
        out_specs=[pl.BlockSpec((256, part), lambda i, w: (i, 0))] * GROUP,
        scratch=[pltpu.VMEM((256, width), F32)],
        flops=2 * length * width * width,
        moved=length * width * 6,
    )(mixer_own, grad_mixed)
    w_out_sum = for_far(w_out_parts[2], w_out_parts[3])
    down_got = swapped(down_theirs, "dp", 1)
    up_got = swapped(up_theirs, "dp", 1)
    gate_sums = first_halved(after(gate_grad, w_out_parts[0]), gate_got, "gate_pair")
    down_sums = first_halved(after(down_grad, gate_sums[0]), down_got, "down_pair")
    gate_z = z_summed(*gate_sums, "gate_half")
    down_z = z_summed(*down_sums, "down_half")
    mixer_got_near = after(mixer_got_far, w_out_sum, down_sums[0])[:, part:]
    grad_mixer_in = [mixer_sent[0], mixer_got_other, mixer_got_far]
    grad_mixer_in += [swapped(mixer_got_near, "group", NEAR)]
    w_out_got = swapped(w_out_sum, "group", FAR)
    w_out_near = swapped(w_out_parts[1], "group", NEAR)
    w_out_grad = (
        w_out_parts[0].astype(F32) + w_out_near.astype(F32) + w_out_got.astype(F32)
    ).astype(BF16)

    taps_f = shape_of((8, part), F32)
    proj_b = shape_of((sequence, 3 * part), BF16)
    last_first = lambda s: pl.BlockSpec((tile, s.shape[1]), lambda i, w: (steps - 1 - i, 0))
    grad_projected, tap_terms, gain_one, *grad_first = call(
        functools.partial(mixer_back_kernel, tiles=tiles, part=part),
        "mixer_back",
        [proj_b, taps_f, row_f] + [block_b] * GROUP,
        where=where,
        grid=(steps,),
        in_specs=[pl.BlockSpec((tile, part), in_block(k, True)) for k in range(GROUP)]
        + [pl.BlockSpec((tile, width), in_block(k, True)) for k in range(GROUP)]
        + [last_first(projected), last_first(convolved)]
        + wholes([small_all, w_in]),
        out_specs=[last_first(proj_b), whole(taps_f), whole(row_f)]
        + [pl.BlockSpec((tile, width), in_block(k, True)) for k in range(GROUP)],
        scratch=[
            pltpu.VMEM((tile, part), BF16),
            pltpu.VMEM((tile, width), BF16),
            pltpu.VMEM((8, part), F32),
        ],
        flops=2 * sequence * width * 3 * part,
        moved=sequence * width * 10,
    )(
        *grad_mixer_in,
        *tokens_of,
        projected,
        convolved,
        after(small_all, gate_sums[0]),
        w_in,
    )

    mixer_mine, mixer_theirs = weight_grad(
        [first_in],
        [after(grad_projected, gate_sums[0], down_sums[0])],
        [(0, k * length, ((0, k * length),), length) for k in range(GROUP)],
        "in_grad",
        more=w_out_grad,
    )
    mixer_got = swapped(after(mixer_theirs, up_got), "dp", 1)
    hold = (mixer_mine, up_got)
    out_got = swapped(after(out_sum, *hold), "group", FAR)
    first_sum = for_far(grad_first[2], after(grad_first[3], *hold))
    first_got = swapped(first_sum, "group", FAR)
    first_near = swapped(after(grad_first[1], *hold), "group", NEAR)
    up_sums = first_halved(after(up_grad, first_sum, first_near), up_got, "up_pair")
    up_z = z_summed(*up_sums, "up_half")
    mixer_sums = halved(
        after(mixer_mine, up_sums[0], gate_z[1], down_z[1]), mixer_got, "mixer_pair"
    )
    mixer_z = z_summed(*mixer_sums, "mixer_half")
    ffn_grads = to_owners([gate_z, up_z, down_z], "ffn")

    block_out = residual + (out_0.astype(F32) + out_near.astype(F32) + out_got.astype(F32))

    tokens_grad = call(
        tokens_grad_kernel,
        "tokens_grad",
        block_f,
        where=where,
        grid=(tiles,),
        in_specs=[by_tile(s) for s in (block_b, block_b, block_b, block_b, block_f)]
        + [whole(small_all)],
        out_specs=by_tile(block_f),
        flops=0,
        moved=length * width * 16,
    )(grad_first[0], first_near, first_got, tokens, grad_resid, small_all)

    mixer_z[0] = after(mixer_z[0], ffn_grads[0], tokens_grad, block_out)
    mixer_grads = to_owners([mixer_z], "mixer")
    mixer_grads = [grad.reshape(owned, width) for grad in mixer_grads]

    gains = jnp.concatenate([gain_one, gain_two], axis=0).reshape(2, GROUP, part)
    gains = [
        lax.dynamic_index_in_dim(gains, where[0] ^ k, 1, keepdims=False) for k in range(GROUP)
    ]
    near = jnp.concatenate([after(gains[1], mixer_grads[0]), gains[3]], axis=0)
    near = jnp.concatenate([gains[0], gains[2]], axis=0) + swapped(near, "group", NEAR)
    small_grad = jnp.concatenate([near[:2] + swapped(near[2:], "group", FAR), tap_terms[:3]], axis=0)
    distance = 1
    while distance < count:
        small_grad = small_grad + swapped(small_grad, "dp", distance)
        distance *= 2

    states = [mixer_master, mixer_first, mixer_second]
    mixer_f, mixer_s, mixer_n = call(
        functools.partial(mixer_adam_kernel, part=part),
        "mixer_adam",
        [shape_of(mixer_master.shape, F32)] * 3,
        where=where,
        in_specs=wholes(mixer_grads + states),
        out_specs=wholes(states),
        scratch=[pltpu.VMEM(mixer_master.shape, F32)],
        flops=0,
        moved=owned * width * 4 * 26,
    )(*mixer_grads, *states)

    states = [ffn_flat, ffn_first.transpose(1, 0, 2), ffn_second.transpose(1, 0, 2)]
    plane = pl.BlockSpec((1, owned, hidden), lambda i, w: (i, 0, 0))
    ffn_new = call(
        functools.partial(ffn_adam_kernel, part=hpart),
        "ffn_adam",
        [shape_of(ffn_flat.shape, F32)] * 3,
        where=where,
        grid=(3,),
        in_specs=[pl.BlockSpec((None, owned, hpart), lambda i, w: (i, 0, 0))] * GROUP + [plane] * 3,
        out_specs=[plane] * 3,
        scratch=[pltpu.VMEM((owned, hidden), F32)],
        flops=0,
        moved=owned * hidden * 3 * 26,
    )(*ffn_grads, *states)
    ffn_f, ffn_s, ffn_n = [new.transpose(1, 0, 2) for new in ffn_new]

    small_f, small_s, small_n = adamw(
        small_master, small_first, small_second, small_grad, rate_small, 0.0
    )

    return (
        block_out,
        tokens_grad,
        mixer_f,
        mixer_s,
        mixer_n,
        ffn_f,
        ffn_s,
        ffn_n,
        small_f,
        small_s,
        small_n,
    )


def solution(mesh):
    both = ("dp", "group")
    matrix = P(both, None)
    stack = P(both, None, None)
    small = P(None, "group")
    in_specs = (matrix, P("dp"), matrix) + (matrix,) * 3 + (stack,) * 3 + (small,) * 3
    out_specs = (matrix, matrix) + (matrix,) * 3 + (stack,) * 3 + (small,) * 3
    return jax.shard_map(local, mesh=mesh, in_specs=in_specs, out_specs=out_specs, check_vma=False)
```

```python
import functools

import jax
import jax.numpy as jnp
from jax import lax
from jax.experimental import pallas as pl
from jax.experimental.pallas import tpu as pltpu
from jax.sharding import PartitionSpec as P

STEP = 10

norm_eps = 1e-06
beta_one = 0.9
beta_two = 0.95
adam_eps = 1e-08
decay_rate = 0.1
rate_matrix = 0.02
rate_small = 1.0

MIB = 1 << 20
ORDER = ((0, 5), (0, 10), (3, 10), (29, 30), (26, 34), (37, 43), (40, 43), (39, 46), (50, 51), (40, 56), (44, 57), (40, 63), (61, 65), (56, 66), (62, 70), (53, 74), (68, 74), (72, 75), (79, 83))
OFF = ((3, 2), (4, 0), (5, 0), (12, 0), (15, 2), (17, 0), (19, 0))
trace = None
VMEM = 60
WEIGHT = 0.001
BF16 = jnp.bfloat16
F32 = jnp.float32
GROUP = 4
NEAR, FAR = 1, 2


def shape_of(shape, dtype):
    return jax.ShapeDtypeStruct(tuple(shape), dtype)


def dot_rows(left, right):
    return lax.dot_general(left, right, (((0,), (0,)), ((), ())), preferred_element_type=F32)


def dot_cols(left, right):
    return lax.dot_general(left, right, (((1,), (1,)), ((), ())), preferred_element_type=F32)


def dot(left, right):
    return jnp.dot(left, right, preferred_element_type=F32)


def adamw(master, first, second, grad, rate, decay):
    first_new = beta_one * first + (1.0 - beta_one) * grad
    second_new = beta_two * second + (1.0 - beta_two) * grad * grad
    fix_one = 1.0 - beta_one**STEP
    fix_two = 1.0 - beta_two**STEP
    direction = first_new / fix_one / (jnp.sqrt(second_new / fix_two) + adam_eps)
    return (first_new, second_new, master - rate * (direction + decay * master))


class Trace:
    def __init__(self):
        self.results = []
        self.holds = 0

    def ready(self, operand):
        step = len(self.results)
        earlier = [self.results[j] for j, i in ORDER if i == step and j < step]
        return lax.optimization_barrier([operand] + earlier)[0] if earlier else operand

    def done(self, results):
        self.results.append(jax.tree.leaves(results)[-1])
        return results


def swapped(block, axis, distance):
    pairs = [(i, i ^ distance) for i in range(lax.axis_size(axis))]
    return trace.done(lax.ppermute(trace.ready(block), axis, pairs))


def after(values, *others):
    hold = trace.holds
    trace.holds += 1
    others = tuple(o for j, o in enumerate(others) if (hold, j) not in OFF)
    return lax.optimization_barrier((values,) + others)[0] if others else values


def call(
    kernel, name, out_shape, *, where, grid=(), in_specs, out_specs, scratch=(), flops, moved, aliases={}
):
    run = pl.pallas_call(
        kernel,
        out_shape=out_shape,
        grid_spec=pltpu.PrefetchScalarGridSpec(
            num_scalar_prefetch=1,
            grid=grid,
            in_specs=in_specs,
            out_specs=out_specs,
            scratch_shapes=scratch,
        ),
        compiler_params=pltpu.CompilerParams(
            vmem_limit_bytes=VMEM * MIB,
            dimension_semantics=("arbitrary",) * len(grid) if grid else None,
        ),
        cost_estimate=pl.CostEstimate(
            flops=int(flops * WEIGHT), bytes_accessed=int(moved * WEIGHT), transcendentals=0
        ),
        input_output_aliases=aliases,
        name=name,
    )
    return lambda first, *rest: trace.done(run(where, trace.ready(first), *rest))


def whole(array):
    rank = len(array.shape)
    return pl.BlockSpec(tuple(array.shape), lambda *_: (0,) * rank)


def wholes(arrays):
    return [whole(a) for a in arrays]


def untouched():
    return pl.BlockSpec(memory_space=pl.ANY)


def send_kernel(where, mixer, ffn, small, *outs, part, hpart, chunks):
    me = where[0]
    base = 4 * part
    last = base + 3 * hpart
    for k in range(GROUP):
        out = outs[k]
        for j in range(4):
            start = pl.multiple_of((me ^ k) * part + j * GROUP * part, part)
            out[:, j * part : (j + 1) * part] = mixer[:, pl.ds(start, part)].astype(BF16)
        for first, size in chunks:
            start = pl.multiple_of((me ^ k) * hpart + first, 128)
            for j in range(3):
                at = base + 3 * first + j * size
                out[:, at : at + size] = ffn[j, :, pl.ds(start, size)].astype(BF16)
        pad = jnp.zeros((out.shape[0] - small.shape[0], part), F32)
        out[:, last:] = jnp.concatenate([small[...], pad], axis=0).astype(BF16)


def take_kernel(where, *refs, part, hpart, chunks):
    blocks, (mixer, small), ffns = refs[:GROUP], refs[GROUP : GROUP + 2], refs[GROUP + 2 :]
    base = 4 * part
    last = base + 3 * hpart
    for k in range(GROUP):
        source = where[0] ^ k
        mixer[source] = blocks[k][:, :base]
        for out, (first, size) in zip(ffns, chunks):
            out[source] = blocks[k][:, base + 3 * first : base + 3 * (first + size)]
        small[:, pl.ds(pl.multiple_of(source * part, part), part)] = blocks[k][:, last:].astype(F32)[
            :8
        ]


def out_stack_kernel(where, *refs, start, size):
    pieces, (out, sems) = refs[:-2], refs[-2:]
    fetch_rows(where, pieces, out, sems, start, size)


def fetch_rows(where, pieces, target, sems, first, cols):
    rows = pieces[0].shape[0]
    copies = [
        pltpu.make_async_copy(
            piece.at[:, pl.ds(first, cols)],
            target.at[pl.ds(pl.multiple_of((where[1] ^ e) * rows, 32), rows), :],
            sems.at[e],
        )
        for e, piece in enumerate(pieces)
    ]
    for copy in copies:
        copy.start()
    for copy in copies:
        copy.wait()


def same_document(where, place, lag):
    same = place >= lag
    for begin in (where[2], where[3]):
        same = jnp.logical_and(same, jnp.logical_or(place < begin, place >= begin + lag))
    return same


def mixer_in_kernel(where, *refs, count, tiles, part):
    tokens, small, refs = refs[:GROUP], refs[GROUP], refs[GROUP + 1 :]
    pieces, refs = refs[:count], refs[count:]
    first_in, projected, convolved, mixer_in, w_in, held, carry, sems = refs
    step = pl.program_id(0)
    me = where[0]

    @pl.when(step == 0)
    def _():
        fetch_rows(where, pieces, w_in, sems, 0, 3 * part)
        carry[...] = jnp.zeros_like(carry)

    for k in range(GROUP):

        @pl.when((step // tiles) ^ me == k)
        def _(k=k):
            held[...] = tokens[k][...]

    inputs = held[...].astype(F32)
    scale = lax.rsqrt(jnp.mean(inputs * inputs, axis=-1, keepdims=True) + norm_eps)
    normed = (inputs * scale * small[0:1, :]).astype(BF16)
    first_in[...] = normed
    columns = dot(normed, w_in[...])
    projected[...] = columns
    gated = (columns[:, :part] * columns[:, 2 * part :]).astype(BF16).astype(F32)
    taps = small[2:5, pl.ds(pl.multiple_of(me * part, part), part)]
    row = lax.broadcasted_iota(jnp.int32, gated.shape, 0)
    before = carry[...]
    one = jnp.where(row == 0, before[7:8], pltpu.roll(gated, 1, 0))
    two = jnp.where(
        row == 0, before[6:7], jnp.where(row == 1, before[7:8], pltpu.roll(gated, 2, 0))
    )
    carry[...] = gated[gated.shape[0] - 8 :]
    place = row + step * gated.shape[0]
    one = jnp.where(same_document(where, place, 1), one, 0.0)
    two = jnp.where(same_document(where, place, 2), two, 0.0)
    mixed = taps[0:1] * gated + taps[1:2] * one + taps[2:3] * two
    convolved[...] = mixed
    mixer_in[...] = (columns[:, part : 2 * part] * mixed).astype(BF16)


def residual_kernel(where, *refs, tiles, part):
    tokens, mixer_in, refs = refs[:GROUP], refs[GROUP : 2 * GROUP], refs[2 * GROUP :]
    small, slices, refs = refs[0], refs[1 : 1 + GROUP], refs[1 + GROUP :]
    second_in, residual_out, mixer_own, w_out, held, inputs_held, sems = refs
    step = pl.program_id(0)
    columns = [pl.ds(pl.multiple_of((where[0] ^ k) * part, part), part) for k in range(GROUP)]

    @pl.when(step == 0)
    def _():
        copies = [
            pltpu.make_async_copy(slices[k], w_out.at[:, columns[k]], sems.at[k])
            for k in range(GROUP)
        ]
        for copy in copies:
            copy.start()
        for copy in copies:
            copy.wait()

    for k in range(GROUP):
        held[:, columns[k]] = mixer_in[k][...]

        @pl.when(step // tiles == k)
        def _(k=k):
            inputs_held[...] = tokens[k][...]

    residual = inputs_held[...].astype(F32) + dot(held[...], w_out[...])
    scale = lax.rsqrt(jnp.mean(residual * residual, axis=-1, keepdims=True) + norm_eps)
    second_in[...] = (residual * scale * small[1:2, :]).astype(BF16)

    @pl.when(step < tiles)
    def _():
        residual_out[...] = residual
        mixer_own[...] = held[...]


def ffn_kernel(where, *refs, tiles, part):
    many = 2 * tiles
    second_in, cots, source, refs = refs[0], refs[1 : 1 + many], refs[1 + many], refs[-11:]
    act_out, gate_out, up_out, cot_out, out_a, out_b, back_a, back_b, weights, held, sem = refs
    step = pl.program_id(0)

    @pl.when(step == 0)
    def _():
        copy = pltpu.make_async_copy(source, weights, sem)
        copy.start()
        copy.wait()

    for k in range(many):

        @pl.when(step == k)
        def _(k=k):
            held[...] = cots[k][...]

    normed = second_in[...]
    cotangent = held[...]
    cot_out[...] = cotangent
    for first in range(0, part, 256):
        size = min(256, part - first)
        gate = dot(normed, weights[:, first : first + size])
        up = dot(normed, weights[:, part + first : part + first + size])
        grad_act = dot(cotangent, weights[:, 2 * part + first : 2 * part + first + size])
        sig = 0.5 * jnp.tanh(0.5 * gate) + 0.5
        swish = gate * sig
        act_out[:, first : first + size] = (swish * up).astype(BF16)
        gate_out[:, first : first + size] = (
            grad_act * up * (sig * (1.0 + gate * (1.0 - sig)))
        ).astype(BF16)
        up_out[:, first : first + size] = (grad_act * swish).astype(BF16)
    out = dot_cols(act_out[...], weights[:, 2 * part :]).astype(BF16)
    back = (
        dot_cols(gate_out[...], weights[:, :part])
        + dot_cols(up_out[...], weights[:, part : 2 * part])
    ).astype(BF16)

    @pl.when(step < tiles)
    def _():
        out_a[...] = out
        back_a[...] = back

    @pl.when(step >= tiles)
    def _():
        out_b[...] = out
        back_b[...] = back


def weight_grad_kernel(where, *refs, lefts, rights, plan, rows, extra):
    left_refs, right_refs, refs = refs[:lefts], refs[lefts : lefts + rights], refs[lefts + rights :]
    if extra:
        (more,), refs = refs[:1], refs[1:]
    many = len(plan[0][2])
    outs, (left_held, right_held, total, sems) = refs[: 2 * many], refs[2 * many :]
    cols = total.shape[2]
    dp = where[1]

    def copies(at):
        left, left_start, sides, size = plan[at]
        slot = at % 2
        return [
            pltpu.make_async_copy(
                left_refs[left].at[pl.ds(left_start, size), :], left_held.at[slot], sems.at[0, slot]
            )
        ] + [
            pltpu.make_async_copy(
                right_refs[right].at[pl.ds(start, size), :],
                right_held.at[slot, m],
                sems.at[1 + m, slot],
            )
            for m, (right, start) in enumerate(sides)
        ]

    for copy in copies(0):
        copy.start()
    for at in range(len(plan)):
        if at + 1 < len(plan):
            for copy in copies(at + 1):
                copy.start()
        for copy in copies(at):
            copy.wait()
        left = left_held[at % 2]
        for m in range(many):
            part = dot_rows(left, right_held[at % 2, m])
            total[m] = part if at == 0 else total[m] + part
    for m in range(many):
        mine, theirs = outs[2 * m : 2 * m + 2]
        for j in range(mine.shape[0]):
            for target, side in ((mine, dp % 2), (theirs, 1 - dp % 2)):
                place = pl.multiple_of((2 * (j ^ (dp // 2)) + side) * rows, 32)
                target[j, :, :cols] = total[m, pl.ds(place, rows), :].astype(BF16)
                if extra:
                    target[j, :, cols:] = more[pl.ds(place, rows), :]


def out_grad_kernel(where, left, right, *refs, part):
    outs, held = refs[:GROUP], refs[GROUP]
    held[...] = dot_rows(left[...], right[...])
    for k in range(GROUP):
        outs[k][...] = held[:, pl.ds(pl.multiple_of((where[0] ^ k) * part, part), part)].astype(BF16)


def first_halve_kernel(where, mine_keep, mine_send, got_keep, got_send, keep, send):
    keep[...] = (mine_keep[...].astype(F32) + got_keep[...].astype(F32)).astype(BF16)
    send[...] = (mine_send[...].astype(F32) + got_send[...].astype(F32)).astype(BF16)


def halve_kernel(where, mine, got, keep, send):
    for j in range(keep.shape[0]):
        keep[j] = (mine[2 * j].astype(F32) + got[2 * j].astype(F32)).astype(BF16)
        send[j] = (mine[2 * j + 1].astype(F32) + got[2 * j + 1].astype(F32)).astype(BF16)


def finish_sum_kernel(where, *refs, terms, owned):
    outs, held = refs[-GROUP - 1 : -1], refs[-1]
    at = 0
    place = 0
    cols = held.shape[2]
    for many in terms:
        for first in range(0, refs[at].shape[1], cols):
            total = refs[at][:, first : first + cols].astype(F32)
            for other in refs[at + 1 : at + many]:
                total = total + other[:, first : first + cols].astype(F32)
            held[...] = total.reshape(held.shape)
            for k in range(GROUP):
                outs[k][place] = held[where[0] ^ k].astype(BF16)
            place += 1
        at += many


def residual_back_kernel(where, g0, g1, g2, residual, cotangent, small, w_out, *refs, part):
    grad_out, mixed_out, gain, outs, held = refs[0], refs[1], refs[2], refs[3:6], refs[6]
    grad = g0[...].astype(F32) + g1[...].astype(F32) + g2[...].astype(F32)
    values = residual[...]
    scale = lax.rsqrt(jnp.mean(values * values, axis=-1, keepdims=True) + norm_eps)
    normed = values * scale
    hat = grad * small[1:2, :]
    grad_in = cotangent[...].astype(F32) + scale * (
        hat - normed * jnp.mean(hat * normed, axis=-1, keepdims=True)
    )
    grad_out[...] = grad_in
    mixed = grad_in.astype(BF16)
    mixed_out[...] = mixed

    @pl.when(pl.program_id(0) == 0)
    def _():
        gain[...] = jnp.zeros_like(gain)

    gain[...] += jnp.sum(grad * normed, axis=0, keepdims=True)
    held[...] = dot_cols(mixed, w_out[...]).astype(BF16)
    for k in range(GROUP):
        columns = held[:, pl.ds(pl.multiple_of((where[0] ^ k) * part, part), part)]
        if k < FAR:
            outs[k][...] = columns
        else:
            outs[FAR][:, (k - FAR) * part : (k - FAR + 1) * part] = columns


def mixer_back_kernel(where, *refs, tiles, part):
    grads, tokens, refs = refs[:GROUP], refs[GROUP : 2 * GROUP], refs[2 * GROUP :]
    (projected, convolved, small, w_in), refs = refs[:4], refs[4:]
    grad_proj, tap_terms, gain, outs, (held, tokens_held, carry) = (
        refs[0],
        refs[1],
        refs[2],
        refs[3 : 3 + GROUP],
        refs[3 + GROUP :],
    )
    step = pl.program_id(0)
    me = where[0]
    which = ((pl.num_programs(0) - 1 - step) // tiles) ^ me

    @pl.when(step == 0)
    def _():
        carry[...] = jnp.zeros_like(carry)
        tap_terms[...] = jnp.zeros_like(tap_terms)
        gain[...] = jnp.zeros_like(gain)

    for k in range(GROUP):

        @pl.when(which == k)
        def _(k=k):
            held[...] = grads[k][...]
            tokens_held[...] = tokens[k][...]

    grad_mixer_in = held[...].astype(F32)
    first_gate = projected[:, :part]
    output_gate = projected[:, part : 2 * part]
    values_in = projected[:, 2 * part :]
    gated = (first_gate * values_in).astype(BF16).astype(F32)
    grad_conv = (grad_mixer_in * output_gate).astype(BF16).astype(F32)
    grad_output = grad_mixer_in * convolved[...]
    size = grad_conv.shape[0]
    row = lax.broadcasted_iota(jnp.int32, grad_conv.shape, 0)
    behind = carry[...]
    one = jnp.where(row == size - 1, behind[0:1], pltpu.roll(grad_conv, size - 1, 0))
    two = jnp.where(
        row == size - 1,
        behind[1:2],
        jnp.where(row == size - 2, behind[0:1], pltpu.roll(grad_conv, size - 2, 0)),
    )
    carry[...] = grad_conv[:8]
    place = row + (pl.num_programs(0) - 1 - step) * size
    last = pl.num_programs(0) * size
    one = jnp.where(jnp.logical_and(same_document(where, place + 1, 1), place + 1 < last), one, 0.0)
    two = jnp.where(jnp.logical_and(same_document(where, place + 2, 2), place + 2 < last), two, 0.0)
    taps = small[2:5, pl.ds(pl.multiple_of(me * part, part), part)]
    grad_gated = taps[0:1] * grad_conv + taps[1:2] * one + taps[2:3] * two
    tap_terms[0:1, :] += jnp.sum(grad_conv * gated, axis=0, keepdims=True)
    tap_terms[1:2, :] += jnp.sum(one * gated, axis=0, keepdims=True)
    tap_terms[2:3, :] += jnp.sum(two * gated, axis=0, keepdims=True)
    grad_proj[:, :part] = (grad_gated * values_in).astype(BF16)
    grad_proj[:, part : 2 * part] = grad_output.astype(BF16)
    grad_proj[:, 2 * part :] = (grad_gated * first_gate).astype(BF16)
    grad_first = dot_cols(grad_proj[...], w_in[...])
    inputs = tokens_held[...].astype(F32)
    scale = lax.rsqrt(jnp.mean(inputs * inputs, axis=-1, keepdims=True) + norm_eps)
    gain[...] += jnp.sum(grad_first * (inputs * scale), axis=0, keepdims=True)
    rounded = grad_first.astype(BF16)
    for k in range(GROUP):

        @pl.when(which == k)
        def _(k=k):
            outs[k][...] = rounded


def tokens_grad_kernel(where, g0, g1, g2, tokens, grad_resid, small, out):
    grad = g0[...].astype(F32) + g1[...].astype(F32) + g2[...].astype(F32)
    values = tokens[...].astype(F32)
    scale = lax.rsqrt(jnp.mean(values * values, axis=-1, keepdims=True) + norm_eps)
    normed = values * scale
    hat = grad * small[0:1, :]
    out[...] = grad_resid[...] + scale * (
        hat - normed * jnp.mean(hat * normed, axis=-1, keepdims=True)
    )


def mixer_adam_kernel(where, g0, g1, g2, g3, master, first, second, first_out, second_out, new_out, held, *, part):
    for k, grad in enumerate((g0, g1, g2, g3)):
        for j in range(4):
            start = (where[0] ^ k) * part + j * GROUP * part
            held[:, pl.ds(pl.multiple_of(start, part), part)] = grad[
                :, j * part : (j + 1) * part
            ].astype(F32)
    first_out[...], second_out[...], new_out[...] = adamw(
        master[...], first[...], second[...], held[...], rate_matrix, decay_rate
    )


def ffn_adam_kernel(where, g0, g1, g2, g3, master, first, second, first_out, second_out, new_out, held, *, part):
    for k, grad in enumerate((g0, g1, g2, g3)):
        start = pl.multiple_of((where[0] ^ k) * part, 128)
        held[:, pl.ds(start, part)] = grad[...].astype(F32)
    first_out[0], second_out[0], new_out[0] = adamw(
        master[0], first[0], second[0], held[...], rate_matrix, decay_rate
    )


def local(
    tokens,
    segments,
    cotangent,
    mixer_master,
    mixer_first,
    mixer_second,
    ffn_master,
    ffn_first,
    ffn_second,
    small_master,
    small_first,
    small_second,
):
    global trace
    trace = Trace()
    length, width = tokens.shape
    hidden = ffn_master.shape[2]
    owned = mixer_master.shape[0]
    count = lax.axis_size("dp")
    sequence = GROUP * length
    part = width // GROUP
    hpart = hidden // GROUP
    rows = GROUP * owned
    tile = length // 2
    tiles = length // tile
    steps = sequence // tile
    chunks = ((0, hpart),)
    where = jnp.stack([lax.axis_index("group"), lax.axis_index("dp")]).astype(jnp.int32)

    def group_gathered(own, *order, then=()):
        far = swapped(after(own, *order) if order else own, "group", FAR)
        near = swapped(own, "group", NEAR)
        return [own, near, far, swapped(after(far, *then) if then else far, "group", NEAR)]

    ffn_flat = ffn_master.transpose(1, 0, 2)
    send = [shape_of((owned, 4 * part + 3 * hpart + part), BF16)] * GROUP
    blocks = call(
        functools.partial(send_kernel, part=part, hpart=hpart, chunks=chunks),
        "send",
        send,
        where=where,
        in_specs=wholes([mixer_master, ffn_flat, small_master]),
        out_specs=wholes(send),
        flops=0,
        moved=owned * (width * 24 + hidden * 18),
    )(mixer_master, ffn_flat, small_master)
    blocks = [blocks[0]] + [swapped(blocks[k], "group", k) for k in range(1, GROUP)]
    take = [shape_of((GROUP, owned, 4 * part), BF16), shape_of((8, width), F32)]
    take += [shape_of((GROUP, owned, 3 * size), BF16) for _, size in chunks]
    mixer_rows, small_all, *ffn_rows = call(
        functools.partial(take_kernel, part=part, hpart=hpart, chunks=chunks),
        "take",
        take,
        where=where,
        in_specs=wholes(blocks),
        out_specs=wholes(take),
        flops=0,
        moved=owned * (width * 16 + hidden * 12),
    )(*blocks)
    far = count // 2

    def z_stages(own):
        pieces = {0: own}
        for e in sorted(range(2, count, 2), key=lambda e: (e.bit_count(), -e)):
            source = pieces[e & (e - 1)]
            pieces[e] = swapped(source, "dp", e & -e)
        return pieces

    mixer_own_rows = mixer_rows.reshape(rows, 4 * part)
    ffn_own_rows = [block.reshape(rows, block.shape[2]) for block in ffn_rows]
    mixer_z = z_stages(mixer_own_rows)
    mixer_near = swapped(mixer_own_rows, "dp", 1)
    mixer_z = lax.optimization_barrier([mixer_z[e] for e in range(2, count, 2)] + [mixer_near])
    mixer_z = mixer_z[: far - 1]
    ffn_cols = lax.all_gather(
        lax.optimization_barrier((ffn_own_rows[0], mixer_z[0], mixer_z[1]))[0], "dp", axis=0, tiled=True
    )
    mixer_x = [swapped(block, "dp", 1) for block in mixer_z]
    mixer_pieces = [mixer_own_rows, mixer_near]
    for block, other in zip(mixer_z, mixer_x):
        mixer_pieces += [block, other]

    tokens_far = swapped(after(tokens, *blocks[1:]), "group", FAR)
    tokens_of = [tokens, swapped(tokens, "group", NEAR), tokens_far]
    tokens_of += [swapped(after(tokens_far, *mixer_x), "group", NEAR)]

    begins = jnp.sum(
        segments[None, :] < jnp.array([[1], [2]], segments.dtype), axis=1, dtype=jnp.int32
    )
    where = jnp.concatenate([where, begins])

    out_stack = shape_of((width, part), BF16)
    out_stacked = call(
        functools.partial(out_stack_kernel, start=3 * part, size=part),
        "stack",
        out_stack,
        where=where,
        in_specs=[untouched()] * count,
        out_specs=whole(out_stack),
        scratch=[pltpu.SemaphoreType.DMA((count,))],
        flops=0,
        moved=width * part * 4,
    )(*mixer_pieces)
    out_slices = [out_stacked, swapped(out_stacked, "group", NEAR), swapped(out_stacked, "group", FAR)]

    def in_block(k, backward=False):
        def place(step, where):
            at = (steps - 1 - step) if backward else step
            return (jnp.clip(at - (where[0] ^ k) * tiles, 0, tiles - 1), 0)

        return place

    outs = [
        shape_of((sequence, width), BF16),
        shape_of((sequence, 3 * part), F32),
        shape_of((sequence, part), F32),
        shape_of((sequence, part), BF16),
        shape_of((width, 3 * part), BF16),
    ]
    forward = lambda s: pl.BlockSpec((tile, s.shape[1]), lambda i, w: (i, 0))
    first_in, projected, convolved, mixer_in, w_in = call(
        functools.partial(mixer_in_kernel, count=count, tiles=tiles, part=part),
        "mixer_in",
        outs,
        where=where,
        grid=(steps,),
        in_specs=[pl.BlockSpec((tile, width), in_block(k)) for k in range(GROUP)]
        + [whole(small_all)]
        + [untouched()] * count,
        out_specs=[forward(s) for s in outs[:4]] + [whole(outs[4])],
        scratch=[
            pltpu.VMEM((tile, width), BF16),
            pltpu.VMEM((8, part), F32),
            pltpu.SemaphoreType.DMA((count,)),
        ],
        flops=2 * sequence * width * 3 * part,
        moved=sequence * width * 8,
    )(*tokens_of, after(small_all, out_stacked), *mixer_pieces)
    out_slices += [swapped(out_slices[2], "group", NEAR)]
    mixer_in_of = group_gathered(after(mixer_in, out_slices[2]), then=out_slices)

    block_b = shape_of((length, width), BF16)
    outs = [
        shape_of((sequence, width), BF16),
        shape_of((length, width), F32),
        block_b,
        shape_of((width, width), BF16),
    ]
    own_block = pl.BlockSpec((tile, width), lambda i, w: (jnp.minimum(i, tiles - 1), 0))
    second_in, residual, mixer_own, w_out = call(
        functools.partial(residual_kernel, tiles=tiles, part=part),
        "residual",
        outs,
        where=where,
        grid=(steps,),
        in_specs=[
            pl.BlockSpec((tile, width), lambda i, w, k=k: (jnp.clip(i - k * tiles, 0, tiles - 1), 0))
            for k in range(GROUP)
        ]
        + [
            pl.BlockSpec((tile, part), lambda i, w: ((w[0] ^ (i // tiles)) * tiles + i % tiles, 0))
        ]
        * GROUP
        + [whole(small_all)]
        + [untouched()] * GROUP,
        out_specs=[forward(outs[0]), own_block, own_block, whole(outs[3])],
        scratch=[
            pltpu.VMEM((tile, width), BF16),
            pltpu.VMEM((tile, width), BF16),
            pltpu.SemaphoreType.DMA((GROUP,)),
        ],
        flops=2 * sequence * width * width,
        moved=sequence * width * 8,
    )(*tokens_of, *mixer_in_of, small_all, *out_slices)

    low = pl.BlockSpec((tile, width), lambda i, w: (jnp.minimum(i, tiles - 1), 0))
    high = pl.BlockSpec((tile, width), lambda i, w: (jnp.maximum(i - tiles, 0), 0))

    wholes_b = [shape_of((sequence, hpart), BF16)] * 3 + [shape_of((sequence, width), BF16)]

    def ffn_call(second_in, begin, cots, name, kept=()):
        at_tile = lambda s: pl.BlockSpec((tile, s.shape[1]), lambda i, w: (i + begin, 0))
        return call(
            functools.partial(ffn_kernel, tiles=tiles, part=hpart),
            name,
            wholes_b + [block_b] * 4,
            where=where,
            grid=(2 * tiles,),
            in_specs=[at_tile(second_in)]
            + [pl.BlockSpec((tile, width), lambda i, w, at=at: (at, 0)) for _, at in cots]
            + [untouched()] * (1 + len(kept)),
            out_specs=[at_tile(s) for s in wholes_b] + [low, high] * 2,
            scratch=[
                pltpu.VMEM((width, 3 * hpart), BF16),
                pltpu.VMEM((tile, width), BF16),
                pltpu.SemaphoreType.DMA(()),
            ],
            flops=24 * length * width * hpart,
            moved=2 * length * (hpart * 6 + width * 8) + width * hpart * 6,
            aliases={3 + len(cots) + j: j for j in range(len(kept))},
        )(second_in, *[cot for cot, _ in cots], ffn_cols, *kept)

    def for_far(mine, near):
        got = swapped(near, "group", NEAR)
        return (mine.astype(F32) + got.astype(F32)).astype(BF16)

    cotangent_near = swapped(cotangent, "group", NEAR)
    cotangent_far = swapped(after(cotangent, mixer_in_of[2]), "group", FAR)
    *kept, out_0, out_1, back_0, back_1 = ffn_call(
        second_in,
        0,
        [(block, at) for block in (cotangent, cotangent_near) for at in range(tiles)],
        "ffn_own",
    )
    cotangent_far = [
        cotangent_far,
        swapped(lax.optimization_barrier((cotangent_far, out_0))[0], "group", NEAR),
    ]
    hidden_act, grad_gate, grad_up, cotangents, out_2, out_3, back_2, back_3 = ffn_call(
        second_in,
        2 * tiles,
        [(block, at) for block in cotangent_far for at in range(tiles)],
        "ffn_far",
        kept,
    )
    back_near = swapped(back_1, "group", NEAR)
    back_sum = for_far(back_2, back_3)
    back_got = swapped(back_sum, "group", FAR)
    out_sum = for_far(out_2, out_3)
    out_near = swapped(out_1, "group", NEAR)

    def weight_grad(lefts, rights, plan, name, more=None):
        cols = rights[0].shape[1]
        many = len(plan[0][2])
        size = plan[0][3]
        out = shape_of(
            (count // 2, rows, cols + (more.shape[1] if more is not None else 0)), BF16
        )
        return call(
            functools.partial(
                weight_grad_kernel,
                lefts=len(lefts),
                rights=len(rights),
                plan=tuple(plan),
                rows=rows,
                extra=more is not None,
            ),
            name,
            [out] * (2 * many),
            where=where,
            in_specs=[untouched()] * (len(lefts) + len(rights))
            + ([whole(more)] if more is not None else []),
            out_specs=wholes([out] * (2 * many)),
            scratch=[
                pltpu.VMEM((2, size, width), BF16),
                pltpu.VMEM((2, many, size, cols), BF16),
                pltpu.VMEM((many, width, cols), F32),
                pltpu.SemaphoreType.DMA((1 + many, 2)),
            ],
            flops=2 * sequence * width * cols * many,
            moved=sequence * (width + cols * many) * 2,
        )(*lefts, *rights, *([more] if more is not None else []))

    def with_theirs(left, right):
        grad = dot_rows(left, right).astype(BF16)
        blocks = grad.reshape(count // 2, 2, rows, grad.shape[1])
        return grad, lax.dynamic_index_in_dim(blocks, 1 - where[1] % 2, 1, keepdims=False)

    gate_grad, gate_theirs = with_theirs(second_in, after(grad_gate, back_sum, back_near))
    gate_got = swapped(gate_theirs, "dp", 1)
    down_grad, down_theirs = with_theirs(cotangents, after(hidden_act, gate_grad))
    up_grad, up_theirs = with_theirs(second_in, after(grad_up, down_grad))

    def to_owners(matrices, name):
        cols = matrices[0][0].shape[1]
        parts = [part for parts in matrices for part in parts]
        blocks_out = shape_of((sum(p[0].shape[1] for p in matrices) // cols, owned, cols), BF16)
        blocks = call(
            functools.partial(
                finish_sum_kernel, terms=tuple(len(parts) for parts in matrices), owned=owned
            ),
            name + "_finish",
            [blocks_out] * GROUP,
            where=where,
            in_specs=wholes(parts),
            out_specs=[whole(blocks_out)] * GROUP,
            scratch=[pltpu.VMEM((GROUP, owned, cols), F32)],
            flops=0,
            moved=rows * cols * 2 * (len(parts) + 1),
        )(*parts)
        return [blocks[0]] + [swapped(blocks[k], "group", k) for k in range(1, GROUP)]

    def halved(mine, got, name):
        half = shape_of((mine.shape[0] // 2,) + mine.shape[1:], BF16)
        return call(
            halve_kernel,
            name,
            [half, half],
            where=where,
            in_specs=wholes([mine, got]),
            out_specs=wholes([half, half]),
            flops=0,
            moved=mine.size * 6,
        )(mine, got)

    def first_halved(grad, got, name):
        cols = grad.shape[1]
        half = shape_of((count // 4, rows, cols), BF16)

        def mine(bit):
            return pl.BlockSpec(
                (rows, cols),
                lambda j, w: (2 * ((2 * j + bit) ^ (w[1] // 2)) + w[1] % 2, 0),
            )

        def theirs(bit):
            return pl.BlockSpec(
                (None, rows, cols), lambda j, w: ((2 * j + bit) ^ (w[1] // 2), 0, 0)
            )

        out = pl.BlockSpec((None, rows, cols), lambda j, w: (j, 0, 0))
        return call(
            first_halve_kernel,
            name,
            [half, half],
            where=where,
            grid=(count // 4,),
            in_specs=[mine(0), mine(1), theirs(0), theirs(1)],
            out_specs=[out, out],
            flops=0,
            moved=grad.size * 3,
        )(grad, grad, got, got)

    def z_summed(keep, send, name):
        distance = 2
        got = swapped(send, "dp", distance)
        while keep.shape[0] > 1:
            keep, send = halved(keep, got, name)
            distance *= 2
            got = swapped(send, "dp", distance)
        return [keep.reshape(keep.shape[1:]), got.reshape(got.shape[1:])]

    block_f = shape_of((length, width), F32)
    row_f = shape_of((1, width), F32)
    slice_b = shape_of((length, part), BF16)
    pair_b = shape_of((length, 2 * part), BF16)
    by_tile = lambda s: pl.BlockSpec((tile, s.shape[1]), lambda i, w: (i, 0))
    grad_resid, grad_mixed, gain_two, *mixer_sent = call(
        functools.partial(residual_back_kernel, part=part),
        "residual_back",
        [block_f, block_b, row_f, slice_b, slice_b, pair_b],
        where=where,
        grid=(tiles,),
        in_specs=[by_tile(s) for s in (block_b, block_b, block_b, block_f, block_b)]
        + wholes([small_all, w_out]),
        out_specs=[by_tile(block_f), by_tile(block_b), whole(row_f)]
        + [by_tile(s) for s in (slice_b, slice_b, pair_b)],
        scratch=[pltpu.VMEM((tile, width), BF16)],
        flops=2 * length * width * width,
        moved=length * width * 20,
    )(after(back_0, up_grad, out_near), back_near, back_got, residual, cotangent, small_all, w_out)
    mixer_got_far = swapped(mixer_sent[2], "group", FAR)
    mixer_got_other = swapped(mixer_sent[1], "group", NEAR)
    cols_b = shape_of((width, part), BF16)
    w_out_parts = call(
        functools.partial(out_grad_kernel, part=part),
        "out_grad",
        [cols_b] * GROUP,
        where=where,
        grid=(width // 256,),
        in_specs=[pl.BlockSpec((length, 256), lambda i, w: (0, i)), whole(block_b)],
        out_specs=[pl.BlockSpec((256, part), lambda i, w: (i, 0))] * GROUP,
        scratch=[pltpu.VMEM((256, width), F32)],
        flops=2 * length * width * width,
        moved=length * width * 6,
    )(mixer_own, grad_mixed)
    w_out_sum = for_far(w_out_parts[2], w_out_parts[3])
    down_got = swapped(down_theirs, "dp", 1)
    up_got = swapped(up_theirs, "dp", 1)
    gate_sums = first_halved(after(gate_grad, w_out_parts[0]), gate_got, "gate_pair")
    down_sums = first_halved(after(down_grad, gate_sums[0]), down_got, "down_pair")
    gate_z = z_summed(*gate_sums, "gate_half")
    down_z = z_summed(*down_sums, "down_half")
    mixer_got_near = after(mixer_got_far, w_out_sum, down_sums[0])[:, part:]
    grad_mixer_in = [mixer_sent[0], mixer_got_other, mixer_got_far]
    grad_mixer_in += [swapped(mixer_got_near, "group", NEAR)]
    w_out_got = swapped(w_out_sum, "group", FAR)
    w_out_near = swapped(w_out_parts[1], "group", NEAR)
    w_out_grad = (
        w_out_parts[0].astype(F32) + w_out_near.astype(F32) + w_out_got.astype(F32)
    ).astype(BF16)

    taps_f = shape_of((8, part), F32)
    proj_b = shape_of((sequence, 3 * part), BF16)
    last_first = lambda s: pl.BlockSpec((tile, s.shape[1]), lambda i, w: (steps - 1 - i, 0))
    grad_projected, tap_terms, gain_one, *grad_first = call(
        functools.partial(mixer_back_kernel, tiles=tiles, part=part),
        "mixer_back",
        [proj_b, taps_f, row_f] + [block_b] * GROUP,
        where=where,
        grid=(steps,),
        in_specs=[pl.BlockSpec((tile, part), in_block(k, True)) for k in range(GROUP)]
        + [pl.BlockSpec((tile, width), in_block(k, True)) for k in range(GROUP)]
        + [last_first(projected), last_first(convolved)]
        + wholes([small_all, w_in]),
        out_specs=[last_first(proj_b), whole(taps_f), whole(row_f)]
        + [pl.BlockSpec((tile, width), in_block(k, True)) for k in range(GROUP)],
        scratch=[
            pltpu.VMEM((tile, part), BF16),
            pltpu.VMEM((tile, width), BF16),
            pltpu.VMEM((8, part), F32),
        ],
        flops=2 * sequence * width * 3 * part,
        moved=sequence * width * 10,
    )(
        *grad_mixer_in,
        *tokens_of,
        projected,
        convolved,
        after(small_all, gate_sums[0]),
        w_in,
    )

    mixer_mine, mixer_theirs = weight_grad(
        [first_in],
        [after(grad_projected, gate_sums[0], down_sums[0])],
        [(0, k * length, ((0, k * length),), length) for k in range(GROUP)],
        "in_grad",
        more=w_out_grad,
    )
    mixer_got = swapped(after(mixer_theirs, up_got), "dp", 1)
    hold = (mixer_mine, up_got)
    out_got = swapped(after(out_sum, *hold), "group", FAR)
    first_sum = for_far(grad_first[2], after(grad_first[3], *hold))
    first_got = swapped(first_sum, "group", FAR)
    first_near = swapped(after(grad_first[1], *hold), "group", NEAR)
    up_sums = first_halved(after(up_grad, first_sum, first_near), up_got, "up_pair")
    up_z = z_summed(*up_sums, "up_half")
    mixer_sums = halved(
        after(mixer_mine, up_sums[0], gate_z[1], down_z[1]), mixer_got, "mixer_pair"
    )
    mixer_z = z_summed(*mixer_sums, "mixer_half")
    ffn_grads = to_owners([gate_z, up_z, down_z], "ffn")

    block_out = residual + (out_0.astype(F32) + out_near.astype(F32) + out_got.astype(F32))

    tokens_grad = call(
        tokens_grad_kernel,
        "tokens_grad",
        block_f,
        where=where,
        grid=(tiles,),
        in_specs=[by_tile(s) for s in (block_b, block_b, block_b, block_b, block_f)]
        + [whole(small_all)],
        out_specs=by_tile(block_f),
        flops=0,
        moved=length * width * 16,
    )(grad_first[0], first_near, first_got, tokens, grad_resid, small_all)

    mixer_z[0] = after(mixer_z[0], ffn_grads[0], tokens_grad, block_out)
    mixer_grads = to_owners([mixer_z], "mixer")
    mixer_grads = [grad.reshape(owned, width) for grad in mixer_grads]

    gains = jnp.concatenate([gain_one, gain_two], axis=0).reshape(2, GROUP, part)
    gains = [
        lax.dynamic_index_in_dim(gains, where[0] ^ k, 1, keepdims=False) for k in range(GROUP)
    ]
    near = jnp.concatenate([after(gains[1], mixer_grads[0]), gains[3]], axis=0)
    near = jnp.concatenate([gains[0], gains[2]], axis=0) + swapped(near, "group", NEAR)
    small_grad = jnp.concatenate([near[:2] + swapped(near[2:], "group", FAR), tap_terms[:3]], axis=0)
    distance = 1
    while distance < count:
        small_grad = small_grad + swapped(small_grad, "dp", distance)
        distance *= 2

    states = [mixer_master, mixer_first, mixer_second]
    mixer_f, mixer_s, mixer_n = call(
        functools.partial(mixer_adam_kernel, part=part),
        "mixer_adam",
        [shape_of(mixer_master.shape, F32)] * 3,
        where=where,
        in_specs=wholes(mixer_grads + states),
        out_specs=wholes(states),
        scratch=[pltpu.VMEM(mixer_master.shape, F32)],
        flops=0,
        moved=owned * width * 4 * 26,
    )(*mixer_grads, *states)

    states = [ffn_flat, ffn_first.transpose(1, 0, 2), ffn_second.transpose(1, 0, 2)]
    plane = pl.BlockSpec((1, owned, hidden), lambda i, w: (i, 0, 0))
    ffn_new = call(
        functools.partial(ffn_adam_kernel, part=hpart),
        "ffn_adam",
        [shape_of(ffn_flat.shape, F32)] * 3,
        where=where,
        grid=(3,),
        in_specs=[pl.BlockSpec((None, owned, hpart), lambda i, w: (i, 0, 0))] * GROUP + [plane] * 3,
        out_specs=[plane] * 3,
        scratch=[pltpu.VMEM((owned, hidden), F32)],
        flops=0,
        moved=owned * hidden * 3 * 26,
    )(*ffn_grads, *states)
    ffn_f, ffn_s, ffn_n = [new.transpose(1, 0, 2) for new in ffn_new]

    small_f, small_s, small_n = adamw(
        small_master, small_first, small_second, small_grad, rate_small, 0.0
    )

    return (
        block_out,
        tokens_grad,
        mixer_f,
        mixer_s,
        mixer_n,
        ffn_f,
        ffn_s,
        ffn_n,
        small_f,
        small_s,
        small_n,
    )


def solution(mesh):
    both = ("dp", "group")
    matrix = P(both, None)
    stack = P(both, None, None)
    small = P(None, "group")
    in_specs = (matrix, P("dp"), matrix) + (matrix,) * 3 + (stack,) * 3 + (small,) * 3
    out_specs = (matrix, matrix) + (matrix,) * 3 + (stack,) * 3 + (small,) * 3
    return jax.shard_map(local, mesh=mesh, in_specs=in_specs, out_specs=out_specs, check_vma=False)
```
